32 devices in a mesh: req: 8 (over y, x, core), hid: 4 (over z).
Axes of the slice: x: 2, y: 2, z: 4, core: 2. Of those that a mesh axis runs over, the one named last changes fastest.
Arguments:
- tokens: bfloat16 [16, 16, 2, 4096], P('req', 'hid'), may hold values from -6 to 6
- input_gain: float32 [4096], replicated, may hold values from 0.1 to 1.9
- qkv_weight: bfloat16 [4096, 3, 4096], P(None, None, 'hid'), may hold values from -0.09375 to 0.09375
- out_weight: bfloat16 [4096, 4096], P('hid'), may hold values from -0.375 to 0.375
- in_weight: bfloat16 [4096, 16384], P(None, ('req', 'hid')), may hold values from -0.09375 to 0.09375
- down_weight: bfloat16 [16384, 4096], P(('req', 'hid')), may hold values from -0.046875 to 0.046875
- final_gain: float32 [4096], replicated, may hold values from 0.1 to 1.9
- score_weight: bfloat16 [4096], replicated, may hold values from -0.09375 to 0.09375
- prompt_keys: bfloat16 [16, 2048, 4096], P('req', None, 'hid'), may hold values from -260 to 260
- prompt_values: bfloat16 [16, 2048, 4096], P('req', None, 'hid'), may hold values from -6 to 6
- tail_keys: bfloat16 [16, 16, 64, 4096], P('req', None, None, 'hid'), may hold values from -12 to 12
- tail_values: bfloat16 [16, 16, 64, 4096], P('req', None, None, 'hid'), may hold values from -6 to 6
- prompt_lengths: int32 [16], P('req'), may hold values from 1 to 2048
- tail_lengths: int32 [16, 16], P('req'), may hold values from 0 to 64
Outputs:
- next_hidden: bfloat16 [16, 16, 2, 4096], P('req', 'hid')
- sample_scores: float32 [16, 16, 2], P('req', 'hid')
The draws below stay inside these ranges and needn't reach their ends.
Inputs may be any that keep to these rules, and one draw needn't show every extreme that they name: `prompt_lengths`: a request's prompt occupies positions 0 to its length - 1. `tail_lengths`: a sample's tail occupies positions 0 to its length - 1.
All inputs are finite; a program needn't handle non-finite values.
Results may differ from the reference program's by a relative error of at most 0.017.
Values may be sent and summed in bfloat16 or wider, within the bound.
A program may use at most 192 MiB of HBM per device.

```python
import jax
import jax.numpy as jnp
from jax import lax

D = 4096
HEADS = 16
HEAD_DIM = 256
ROT = 64
FF = 16384
SAMPLES = 16
NEW = 2
PROMPT = 2048
TAIL = 64
REQUESTS = 16
TOKENS = 512


def draw_prompt_keys(key, part):
    base_key = jax.random.fold_in(key, 0)
    key_dims = (REQUESTS, PROMPT, D)
    drawn = jnp.clip(jax.random.normal(base_key, key_dims, jnp.float32), -6.0, 6.0) * 2.0
    return drawn.astype(jnp.bfloat16)


def set_ends(result, own_key, least, largest):
    shape = result.shape
    spot = [jax.random.randint(jax.random.fold_in(own_key, axis), (), 0, shape[axis]) for axis in range(len(shape))]
    result = result.at[tuple(spot)].set(least)
    longest = shape.index(max(shape))
    spot[longest] = (spot[longest] + 1) % shape[longest]
    return result.at[tuple(spot)].set(largest)


def levels(own_key, extent, cuts, smallest, largest):
    level = 1.0
    for dim, blocks in cuts:
        heights = jax.random.uniform(jax.random.fold_in(jax.random.fold_in(own_key, 6), dim), (blocks,), jnp.float32, smallest / len(cuts), largest / len(cuts))
        level = level * jnp.repeat(jnp.exp(heights), extent[dim] // blocks).reshape((-1,) + (1,) * (len(extent) - 1 - dim))
    return level


def bell_draw(own_key, extent, deviation, most, shards=(), kind=jnp.bfloat16):
    level = levels(own_key, extent, shards, -0.22, 0.18) if shards else 1.0
    entries = jax.random.normal(own_key, extent, jnp.float32) * deviation * level
    return jnp.minimum(jnp.maximum(entries, -most), most).astype(kind)


def setup_inputs(seed: int = 0) -> dict:
    key_list = jax.random.split(jax.random.key(seed), 15)
    tokens = bell_draw(key_list[0], (REQUESTS, SAMPLES, NEW, D), 1.0, 6.0, ((0, 8), (1, 4)))
    input_gain = jnp.clip(1.0 + 0.18 * jax.random.normal(key_list[1], (D,), jnp.float32), 0.1, 1.9)
    qkv_weight = bell_draw(key_list[2], (D, 3, D), D ** -0.5, 0.09375, ((2, 4),))
    out_weight = bell_draw(key_list[3], (D, D), (D // 16) ** -0.5, 0.375, ((0, 4),))
    in_weight = bell_draw(key_list[4], (D, FF), D ** -0.5, 0.09375, ((1, 32),))
    down_weight = bell_draw(key_list[5], (FF, D), FF ** -0.5, 0.046875, ((0, 32),))
    final_gain = jnp.clip(1.0 + 0.18 * jax.random.normal(key_list[6], (D,), jnp.float32), 0.1, 1.9)
    score_weight = bell_draw(key_list[7], (D,), D ** -0.5, 0.09375)
    prompt_keys = draw_prompt_keys(jax.random.fold_in(key_list[14], 71), 0)
    prompt_values = bell_draw(key_list[9], (REQUESTS, PROMPT, D), 1.0, 6.0, ((0, 8), (2, 4)))
    tail_keys = bell_draw(key_list[10], (REQUESTS, SAMPLES, TAIL, D), 2.0, 12.0, ((0, 8), (3, 4)))
    tail_values = bell_draw(key_list[11], (REQUESTS, SAMPLES, TAIL, D), 1.0, 6.0, ((0, 8), (3, 4)))
    prompt_lengths = set_ends(jax.random.randint(key_list[12], (REQUESTS,), 1, PROMPT + 1), jax.random.fold_in(key_list[12], 1), 1, PROMPT).astype(jnp.int32)
    tail_lengths = set_ends(jax.random.randint(key_list[13], (REQUESTS, SAMPLES), 0, TAIL + 1), jax.random.fold_in(key_list[13], 1), 0, TAIL).astype(jnp.int32)
    return dict(tokens=tokens, input_gain=input_gain, qkv_weight=qkv_weight, out_weight=out_weight, in_weight=in_weight, down_weight=down_weight, final_gain=final_gain, score_weight=score_weight, prompt_keys=prompt_keys, prompt_values=prompt_values, tail_keys=tail_keys, tail_values=tail_values, prompt_lengths=prompt_lengths, tail_lengths=tail_lengths)


very_low = -1e+30

def layer_norm(values, gain):
    centre = lax.optimization_barrier(jnp.mean(values, axis=-1, keepdims=True))
    centred = values - centre
    spread = lax.optimization_barrier(jnp.mean(centred * centred, axis=-1, keepdims=True))
    return centred * lax.rsqrt(spread + 1e-05) * gain

def rotate(vectors, positions):
    half_rot = ROT // 2
    frequency = 10000.0 ** (-(jnp.arange(half_rot, dtype=jnp.float32) * (2.0 / ROT)))
    angles = positions.astype(jnp.float32)[..., None] * frequency
    cosine = jnp.cos(angles)[..., None, :]
    sine_part = jnp.sin(angles)[..., None, :]
    paired = vectors[..., :ROT].reshape(vectors.shape[:-1] + (half_rot, 2))
    even_part = paired[..., 0]
    odd_part = paired[..., 1]
    turned = jnp.stack([even_part * cosine - odd_part * sine_part, odd_part * cosine + even_part * sine_part], axis=-1)
    return jnp.concatenate([turned.reshape(vectors.shape[:-1] + (ROT,)), vectors[..., ROT:]], axis=-1)

def widen(array):
    return array.astype(jnp.float32)

def attend_one(operands):
    queries, new_keys, new_values, cached_keys, cached_values, later_keys, later_values, prompt_len, tail_len = operands
    score_scale = HEAD_DIM ** (-0.5)
    prompt_scores = jnp.einsum('sthd,khd->sthk', widen(queries), widen(cached_keys)) * score_scale
    prompt_keep = (jnp.arange(PROMPT, dtype=jnp.int32) < prompt_len)[None, None, None, :]
    tail_scores = jnp.einsum('sthd,skhd->sthk', widen(queries), widen(later_keys)) * score_scale
    tail_keep = (jnp.arange(TAIL, dtype=jnp.int32)[None, :] < tail_len[:, None])[:, None, None, :]
    self_scores = jnp.einsum('sthd,suhd->sthu', widen(queries), widen(new_keys)) * score_scale
    position_order = jnp.arange(NEW, dtype=jnp.int32)
    self_keep = (position_order[None, :] <= position_order[:, None])[None, :, None, :]
    highest = jnp.maximum(lax.optimization_barrier(jnp.max(jnp.where(prompt_keep, prompt_scores, very_low), axis=-1)), lax.optimization_barrier(jnp.max(jnp.where(tail_keep, tail_scores, very_low), axis=-1)))
    highest = jnp.maximum(highest, lax.optimization_barrier(jnp.max(jnp.where(self_keep, self_scores, very_low), axis=-1)))
    prompt_weights = jnp.where(prompt_keep, jnp.exp(prompt_scores - highest[..., None]), 0.0)
    tail_weights = jnp.where(tail_keep, jnp.exp(tail_scores - highest[..., None]), 0.0)
    self_weights = jnp.where(self_keep, jnp.exp(self_scores - highest[..., None]), 0.0)
    totals = lax.optimization_barrier(jnp.sum(prompt_weights, axis=-1)) + lax.optimization_barrier(jnp.sum(tail_weights, axis=-1)) + lax.optimization_barrier(jnp.sum(self_weights, axis=-1))
    accrued = jnp.einsum('sthk,khd->sthd', widen(prompt_weights.astype(jnp.bfloat16)), widen(cached_values))
    accrued = accrued + jnp.einsum('sthk,skhd->sthd', widen(tail_weights.astype(jnp.bfloat16)), widen(later_values))
    accrued = accrued + jnp.einsum('sthu,suhd->sthd', widen(self_weights.astype(jnp.bfloat16)), widen(new_values))
    return (accrued / totals[..., None]).astype(jnp.bfloat16)

def reference(tokens, input_gain, qkv_weight, out_weight, in_weight, down_weight, final_gain, score_weight, prompt_keys, prompt_values, tail_keys, tail_values, prompt_lengths, tail_lengths):
    residual = tokens.astype(jnp.float32).reshape(TOKENS, D)
    normed = layer_norm(residual, input_gain).astype(jnp.bfloat16)
    mixed_qkv = jnp.dot(normed, qkv_weight.reshape(D, 3 * D), preferred_element_type=jnp.float32).astype(jnp.bfloat16)
    mixed_qkv = mixed_qkv.reshape(REQUESTS, SAMPLES, NEW, 3, HEADS, HEAD_DIM)
    positions = prompt_lengths[:, None, None] + tail_lengths[:, :, None] + jnp.arange(NEW, dtype=jnp.int32)[None, None, :]
    queries = rotate(mixed_qkv[:, :, :, 0].astype(jnp.float32), positions).astype(jnp.bfloat16)
    new_keys = rotate(mixed_qkv[:, :, :, 1].astype(jnp.float32), positions).astype(jnp.bfloat16)
    new_values = mixed_qkv[:, :, :, 2]
    cached_keys = prompt_keys.reshape(REQUESTS, PROMPT, HEADS, HEAD_DIM)
    cached_values = prompt_values.reshape(REQUESTS, PROMPT, HEADS, HEAD_DIM)
    later_keys = tail_keys.reshape(REQUESTS, SAMPLES, TAIL, HEADS, HEAD_DIM)
    later_values = tail_values.reshape(REQUESTS, SAMPLES, TAIL, HEADS, HEAD_DIM)
    attended = lax.map(attend_one, (queries, new_keys, new_values, cached_keys, cached_values, later_keys, later_values, prompt_lengths, tail_lengths))
    attended = attended.reshape(TOKENS, D)
    projected = jnp.dot(attended, out_weight, preferred_element_type=jnp.float32)
    hidden_units = jax.nn.gelu(jnp.dot(normed, in_weight, preferred_element_type=jnp.float32), approximate=True).astype(jnp.bfloat16)
    final_state = residual + projected + jnp.dot(hidden_units, down_weight, preferred_element_type=jnp.float32)
    next_hidden = final_state.astype(jnp.bfloat16).reshape(REQUESTS, SAMPLES, NEW, D)
    sample_scores = lax.optimization_barrier(jnp.sum(layer_norm(final_state, final_gain) * score_weight.astype(jnp.float32), axis=-1))
    return (next_hidden, sample_scores.reshape(REQUESTS, SAMPLES, NEW))
```

```python
import functools

import jax
import jax.numpy as jnp
from jax import lax
from jax.experimental import pallas as pl
from jax.experimental.pallas import tpu as pltpu
from jax.sharding import PartitionSpec as P

HEAD_DIM = 256
ROT = 64


very_low = -1e30


def layer_norm(values, gain):
    centre = jnp.mean(values, axis=-1, keepdims=True)
    centred = values - centre
    spread = jnp.mean(centred * centred, axis=-1, keepdims=True)
    return centred * lax.rsqrt(spread + 1e-05) * gain


def rotate(vectors, positions):
    half_rot = ROT // 2
    frequency = 10000.0 ** (-(jnp.arange(half_rot, dtype=jnp.float32) * (2.0 / ROT)))
    angles = positions.astype(jnp.float32)[..., None] * frequency
    cosine = jnp.cos(angles)[..., None, :]
    sine_part = jnp.sin(angles)[..., None, :]
    paired = vectors[..., :ROT].reshape(vectors.shape[:-1] + (half_rot, 2))
    even_part = paired[..., 0]
    odd_part = paired[..., 1]
    turned = jnp.stack(
        [even_part * cosine - odd_part * sine_part, odd_part * cosine + even_part * sine_part],
        axis=-1,
    )
    return jnp.concatenate(
        [turned.reshape(vectors.shape[:-1] + (ROT,)), vectors[..., ROT:]], axis=-1
    )


CHUNKS = 4
MESH = pl.DeviceIdType.MESH


def flip(index, bit):
    return index + bit * (1 - 2 * lax.rem(lax.div(index, bit), 2))


def place(slot, count):
    return slot // 2 + (slot % 2) * (count // 2)


def greet(bits, hid_count):
    req, hid = lax.axis_index("req"), lax.axis_index("hid")
    barrier = pltpu.get_barrier_semaphore()
    for bit in bits:
        pl.semaphore_signal(barrier, inc=1, device_id=(flip(req, bit), hid), device_id_type=MESH)
    for step in range(1, hid_count):
        other = lax.rem(hid + step, hid_count)
        pl.semaphore_signal(barrier, inc=1, device_id=(req, other), device_id_type=MESH)
    return lambda: pl.semaphore_wait(barrier, len(bits) + hid_count - 1)


def reduce_orders(req_count):
    bits = [1 << i for i in range(req_count.bit_length() - 1)]
    return [bits if c % 2 == 0 else bits[:1] + bits[:0:-1] for c in range(CHUNKS)]


def gather_kernel(
    req_count, hid_count, tok_ref, gain_ref, w_hbm, group_ref, hidden_ref,
    full, w_ref, total, hid_send, hid_recv, req_send, req_recv, w_sem,
):
    req, hid = lax.axis_index("req"), lax.axis_index("hid")
    orders = [order[::-1] for order in reduce_orders(req_count)]
    width = tok_ref.shape[1] // CHUNKS
    half = req_count // 2
    greeted = greet(orders[0], hid_count)
    w_copy = pltpu.make_async_copy(w_hbm, w_ref, w_sem)
    w_copy.start()
    values = tok_ref[...].astype(jnp.float32)
    full[0, hid] = layer_norm(values, gain_ref[...]).astype(full.dtype)
    greeted()
    columns = [pl.ds(c * width, width) for c in range(CHUNKS)]
    sent = []
    arriving = [[] for _ in range(CHUNKS)]
    for c in range(CHUNKS):
        for step in range(1, hid_count):
            block = full.at[0, hid, :, columns[c]]
            copy = pltpu.make_async_remote_copy(
                src_ref=block, dst_ref=block,
                send_sem=hid_send.at[c, step - 1], recv_sem=hid_recv.at[c, step - 1],
                device_id=(req, lax.rem(hid + step, hid_count)), device_id_type=MESH,
            )
            copy.start()
            sent.append(copy)
            arriving[c].append(copy)
    held = [[0] for _ in range(CHUNKS)]
    for stage in range(len(orders[0])):
        for c in range(CHUNKS):
            bit = orders[c][stage]
            for copy in arriving[c]:
                copy.wait_recv()
            arriving[c] = []
            for slot in list(held[c]):
                there = slot ^ bit
                copy = pltpu.make_async_remote_copy(
                    src_ref=full.at[place(slot, req_count), :, :, columns[c]],
                    dst_ref=full.at[place(there, req_count), :, :, columns[c]],
                    send_sem=req_send.at[c, there - 1], recv_sem=req_recv.at[c, there - 1],
                    device_id=(flip(req, bit), hid), device_id_type=MESH,
                )
                copy.start()
                sent.append(copy)
                arriving[c].append(copy)
                held[c].append(there)
        if stage == 0:
            group_ref[...] = full[0]
    w_copy.wait()
    rows = half * full.shape[1] * full.shape[2]
    for side in range(2):
        for c in range(CHUNKS):
            if side == 1:
                for copy in arriving[c]:
                    copy.wait_recv()
            block = full[side * half : (side + 1) * half, :, :, c * width : (c + 1) * width]
            part = jnp.dot(
                block.reshape(rows, width), w_ref[c * width : (c + 1) * width, :],
                preferred_element_type=jnp.float32,
            )
            total[...] = part if c == 0 else total[...] + part
        hidden_ref[side] = jax.nn.gelu(total[...], approximate=True).astype(hidden_ref.dtype)
    for copy in sent:
        copy.wait_send()


def reduce_kernel(
    req_count, hid_count, hidden_ref, proj_ref, w_hbm, out_ref,
    w_ref, part, landed, total, leaving, hid_landed,
    w_sem, req_send, req_recv, hid_send, hid_recv,
):
    req, hid = lax.axis_index("req"), lax.axis_index("hid")
    orders = reduce_orders(req_count)
    half = req_count // 2
    width = part.shape[-1]
    block_shape = (half,) + part.shape[2:]
    greeted = greet(orders[0], hid_count)
    w_copies = []
    for c in range(CHUNKS):
        copy = pltpu.make_async_copy(
            w_hbm.at[:, pl.ds(c * width, width)], w_ref.at[c], w_sem.at[c]
        )
        copy.start()
        w_copies.append(copy)
    sent = []

    def send(c, slot, bit):
        copy = pltpu.make_async_remote_copy(
            src_ref=part.at[c, place(slot, req_count)], dst_ref=landed.at[c, slot - 1],
            send_sem=req_send.at[c, slot - 1], recv_sem=req_recv.at[c, slot - 1],
            device_id=(flip(req, bit), hid), device_id_type=MESH,
        )
        copy.start()
        sent.append(copy)
        return copy

    active = [list(range(req_count)) for _ in range(CHUNKS)]
    arriving = [{} for _ in range(CHUNKS)]
    for c in range(CHUNKS):
        w_copies[c].wait()
        for side in (1, 0):
            value = jnp.dot(hidden_ref[side], w_ref[c], preferred_element_type=jnp.float32)
            part[c, side * half : (side + 1) * half] = value.astype(part.dtype).reshape(block_shape)
            if side == 1:
                if c == 0:
                    greeted()
                for slot in range(1, req_count, 2):
                    arriving[c][slot] = send(c, slot, 1)
        active[c] = list(range(0, req_count, 2))
    for stage in range(1, len(orders[0])):
        for c in range(CHUNKS):
            before, bit = orders[c][stage - 1], orders[c][stage]
            landing, arriving[c] = arriving[c], {}
            for slot in sorted(active[c], key=lambda s: -(s & bit)):
                landing[slot | before].wait_recv()
                at = place(slot, req_count)
                both = part[c, at].astype(jnp.float32) + landed[c, (slot | before) - 1].astype(
                    jnp.float32
                )
                part[c, at] = both.astype(part.dtype)
                if slot & bit:
                    arriving[c][slot] = send(c, slot, bit)
            active[c] = [slot for slot in active[c] if not slot & bit]
    hid_copies = []
    for c in range(CHUNKS):
        last = orders[c][-1]
        arriving[c][last].wait_recv()
        both = part[c, 0].astype(jnp.float32) + landed[c, last - 1].astype(jnp.float32)
        both = both + proj_ref[:, :, c * width : (c + 1) * width]
        total[c] = both
        leaving[c] = both.astype(leaving.dtype)
        for step in range(1, hid_count):
            other = lax.rem(hid + step, hid_count)
            copy = pltpu.make_async_remote_copy(
                src_ref=leaving.at[c, other], dst_ref=hid_landed.at[c, step - 1],
                send_sem=hid_send.at[c, step - 1], recv_sem=hid_recv.at[c, step - 1],
                device_id=(req, other), device_id_type=MESH,
            )
            copy.start()
            sent.append(copy)
            hid_copies.append(copy)
    for c in range(CHUNKS):
        value = total[c, hid]
        for step in range(1, hid_count):
            hid_copies[c * (hid_count - 1) + step - 1].wait_recv()
            value = value + hid_landed[c, step - 1].astype(jnp.float32)
        out_ref[:, c * width : (c + 1) * width] = value
    for copy in sent:
        copy.wait_send()


def in_vmem(count):
    return [pl.BlockSpec(memory_space=pltpu.VMEM)] * count


def params(collective_id):
    return pltpu.CompilerParams(
        collective_id=collective_id, has_side_effects=True, vmem_limit_bytes=48 * 2**20
    )


def gather_up(own_tokens, gain, in_weight):
    req_count, hid_count = lax.axis_size("req"), lax.axis_size("hid")
    rows, width = own_tokens.shape
    units = in_weight.shape[1]
    side_rows = req_count // 2 * hid_count * rows
    dma = pltpu.SemaphoreType.DMA
    return pl.pallas_call(
        functools.partial(gather_kernel, req_count, hid_count),
        out_shape=(
            jax.ShapeDtypeStruct((hid_count, rows, width), jnp.bfloat16),
            jax.ShapeDtypeStruct((2, side_rows, units), jnp.bfloat16),
        ),
        in_specs=in_vmem(2) + [pl.BlockSpec(memory_space=pl.ANY)],
        out_specs=tuple(in_vmem(2)),
        scratch_shapes=[
            pltpu.VMEM((req_count, hid_count, rows, width), jnp.bfloat16),
            pltpu.VMEM((width, units), jnp.bfloat16),
            pltpu.VMEM((side_rows, units), jnp.float32),
            dma((CHUNKS, hid_count - 1)),
            dma((CHUNKS, hid_count - 1)),
            dma((CHUNKS, req_count - 1)),
            dma((CHUNKS, req_count - 1)),
            dma(()),
        ],
        compiler_params=params(0),
        name="gather_up",
    )(own_tokens, gain.reshape(1, width), in_weight)


def down_reduce(hidden_units, projected, down_weight):
    req_count, hid_count = lax.axis_size("req"), lax.axis_size("hid")
    _, rows, width = projected.shape
    units = down_weight.shape[0]
    part_width = width // CHUNKS
    dma = pltpu.SemaphoreType.DMA
    return pl.pallas_call(
        functools.partial(reduce_kernel, req_count, hid_count),
        out_shape=jax.ShapeDtypeStruct((rows, width), jnp.float32),
        in_specs=in_vmem(2) + [pl.BlockSpec(memory_space=pl.ANY)],
        out_specs=in_vmem(1)[0],
        scratch_shapes=[
            pltpu.VMEM((CHUNKS, units, part_width), jnp.bfloat16),
            pltpu.VMEM((CHUNKS, req_count, hid_count, rows, part_width), jnp.bfloat16),
            pltpu.VMEM((CHUNKS, req_count - 1, hid_count, rows, part_width), jnp.bfloat16),
            pltpu.VMEM((CHUNKS, hid_count, rows, part_width), jnp.float32),
            pltpu.VMEM((CHUNKS, hid_count, rows, part_width), jnp.bfloat16),
            pltpu.VMEM((CHUNKS, hid_count - 1, rows, part_width), jnp.bfloat16),
            dma((CHUNKS,)),
            dma((CHUNKS, req_count - 1)),
            dma((CHUNKS, req_count - 1)),
            dma((CHUNKS, hid_count - 1)),
            dma((CHUNKS, hid_count - 1)),
        ],
        compiler_params=params(1),
        name="down_reduce",
    )(hidden_units, projected, down_weight)


def shards(
    tokens,
    input_gain,
    qkv_weight,
    out_weight,
    in_weight,
    down_weight,
    final_gain,
    score_weight,
    prompt_keys,
    prompt_values,
    tail_keys,
    tail_values,
    prompt_lengths,
    tail_lengths,
):
    req_dev, samp_dev, fresh, width = tokens.shape
    own_rows = req_dev * samp_dev * fresh
    own_tokens = tokens.reshape(own_rows, width)
    residual = own_tokens.astype(jnp.float32)
    group_normed, hidden_units = gather_up(own_tokens, input_gain, in_weight)
    slab_rows, triple, slab_cols = qkv_weight.shape
    hid_count = lax.axis_size("hid")
    group_rows = own_rows * hid_count
    mixed_qkv = jnp.einsum(
        "nd,jdc->jnc",
        group_normed.reshape(group_rows, width),
        jnp.transpose(qkv_weight, (1, 0, 2)),
        preferred_element_type=jnp.float32,
    ).astype(jnp.bfloat16)
    mixed_qkv = jnp.transpose(mixed_qkv, (1, 0, 2))
    heads_here = slab_cols // HEAD_DIM
    samples = hid_count * samp_dev
    grouped = mixed_qkv.reshape(hid_count, req_dev, samp_dev, fresh, triple, heads_here, HEAD_DIM)
    grouped = jnp.transpose(grouped, (1, 0, 2, 3, 4, 5, 6)).reshape(
        req_dev, samples, fresh, triple, heads_here, HEAD_DIM
    )
    positions = (
        prompt_lengths[:, None, None]
        + tail_lengths[:, :, None]
        + jnp.arange(fresh, dtype=jnp.int32)[None, None, :]
    )
    queries = rotate(grouped[:, :, :, 0].astype(jnp.float32), positions).astype(jnp.bfloat16)
    new_keys = rotate(grouped[:, :, :, 1].astype(jnp.float32), positions).astype(jnp.bfloat16)
    new_values = grouped[:, :, :, 2]
    prompt_len = prompt_keys.shape[1]
    cached_keys = prompt_keys.reshape(req_dev, prompt_len, heads_here, HEAD_DIM)
    cached_values = prompt_values.reshape(req_dev, prompt_len, heads_here, HEAD_DIM)
    prompt_queries = queries.reshape(req_dev, samples * fresh, heads_here, HEAD_DIM)
    score_scale = HEAD_DIM ** (-0.5)
    prompt_scores = (
        jnp.einsum(
            "rqhd,rkhd->rqhk", prompt_queries, cached_keys, preferred_element_type=jnp.float32
        )
        * score_scale
    )
    keeping = (jnp.arange(prompt_len, dtype=jnp.int32)[None, :] < prompt_lengths[:, None])[
        :, None, None, :
    ]
    prompt_scores = jnp.where(keeping, prompt_scores, very_low)
    peaks = jnp.max(prompt_scores, axis=-1)
    prompt_weights = jnp.where(keeping, jnp.exp(prompt_scores - peaks[..., None]), 0.0)
    totals = jnp.sum(prompt_weights, axis=-1)
    accrued = jnp.einsum(
        "rqhk,rkhd->rqhd",
        prompt_weights.astype(jnp.bfloat16),
        cached_values,
        preferred_element_type=jnp.float32,
    )
    peaks = peaks.reshape(req_dev, samples, fresh, heads_here)
    totals = totals.reshape(req_dev, samples, fresh, heads_here)
    accrued = accrued.reshape(req_dev, samples, fresh, heads_here, HEAD_DIM)
    tail_len = tail_keys.shape[2]
    later_keys = tail_keys.reshape(req_dev, samples, tail_len, heads_here, HEAD_DIM)
    later_values = tail_values.reshape(req_dev, samples, tail_len, heads_here, HEAD_DIM)
    tail_scores = (
        jnp.einsum("rsthd,rskhd->rsthk", queries, later_keys, preferred_element_type=jnp.float32)
        * score_scale
    )
    tail_keep = (jnp.arange(tail_len, dtype=jnp.int32)[None, None, :] < tail_lengths[:, :, None])[
        :, :, None, None, :
    ]
    self_scores = (
        jnp.einsum("rsthd,rsuhd->rsthu", queries, new_keys, preferred_element_type=jnp.float32)
        * score_scale
    )
    position_order = jnp.arange(fresh, dtype=jnp.int32)
    self_keep = (position_order[None, :] <= position_order[:, None])[None, None, :, None, :]
    highest = jnp.maximum(peaks, jnp.max(jnp.where(tail_keep, tail_scores, very_low), axis=-1))
    highest = jnp.maximum(highest, jnp.max(jnp.where(self_keep, self_scores, very_low), axis=-1))
    scaling = jnp.exp(peaks - highest)
    tail_weights = jnp.where(tail_keep, jnp.exp(tail_scores - highest[..., None]), 0.0)
    self_weights = jnp.where(self_keep, jnp.exp(self_scores - highest[..., None]), 0.0)
    totals = totals * scaling + jnp.sum(tail_weights, axis=-1) + jnp.sum(self_weights, axis=-1)
    accrued = accrued * scaling[..., None]
    accrued = accrued + jnp.einsum(
        "rsthk,rskhd->rsthd",
        tail_weights.astype(jnp.bfloat16),
        later_values,
        preferred_element_type=jnp.float32,
    )
    accrued = accrued + jnp.einsum(
        "rsthu,rsuhd->rsthd",
        self_weights.astype(jnp.bfloat16),
        new_values,
        preferred_element_type=jnp.float32,
    )
    attended = (accrued / totals[..., None]).astype(jnp.bfloat16)
    attended = attended.reshape(req_dev, hid_count, samp_dev, fresh, heads_here * HEAD_DIM)
    attended_rows = jnp.transpose(attended, (1, 0, 2, 3, 4)).reshape(
        group_rows, heads_here * HEAD_DIM
    )
    projected = jnp.dot(attended_rows, out_weight, preferred_element_type=jnp.float32)
    branch_sum = down_reduce(
        hidden_units, projected.reshape(hid_count, own_rows, width), down_weight
    )
    final_state = residual + branch_sum
    next_hidden = final_state.astype(jnp.bfloat16).reshape(req_dev, samp_dev, fresh, width)
    sample_scores = jnp.sum(
        layer_norm(final_state, final_gain) * score_weight.astype(jnp.float32), axis=-1
    )
    return (next_hidden, sample_scores.reshape(req_dev, samp_dev, fresh))


def solution(mesh):
    placed = (
        P("req", "hid", None, None),
        P(),
        P(None, None, "hid"),
        P("hid", None),
        P(None, ("req", "hid")),
        P(("req", "hid"), None),
        P(),
        P(),
        P("req", None, "hid"),
        P("req", None, "hid"),
        P("req", None, None, "hid"),
        P("req", None, None, "hid"),
        P("req"),
        P("req", None),
    )
    return jax.shard_map(
        shards,
        mesh=mesh,
        in_specs=placed,
        out_specs=(P("req", "hid", None, None), P("req", "hid", None)),
        check_vma=False,
    )
```

```python
import functools

import jax
import jax.numpy as jnp
from jax import lax
from jax.experimental import pallas as pl
from jax.experimental.pallas import tpu as pltpu
from jax.sharding import PartitionSpec as P

HEAD_DIM = 256
ROT = 64


very_low = -1e30


def layer_norm(values, gain):
    centre = jnp.mean(values, axis=-1, keepdims=True)
    centred = values - centre
    spread = jnp.mean(centred * centred, axis=-1, keepdims=True)
    return centred * lax.rsqrt(spread + 1e-05) * gain


def turn(vectors, table):
    lanes = table.shape[-1]
    first = vectors[:, :lanes]
    even = lax.rem(lax.broadcasted_iota(jnp.int32, first.shape, 1), 2) == 0
    other = jnp.where(even, pltpu.roll(first, lanes - 1, 1), pltpu.roll(first, 1, 1))
    return jnp.concatenate([first * table[0] + other * table[1], vectors[:, lanes:]], axis=1)


def rotation_table(positions):
    lane = jnp.arange(2 * ROT, dtype=jnp.int32)
    frequency = 10000.0 ** (-((lane // 2).astype(jnp.float32) * (2.0 / ROT)))
    angles = positions.astype(jnp.float32)[:, None] * jnp.where(lane < ROT, frequency, 0.0)
    sign = jnp.where(lane % 2 == 0, -1.0, 1.0)
    return jnp.stack([jnp.cos(angles), jnp.sin(angles) * sign])


CHUNKS = 4
MESH = pl.DeviceIdType.MESH


def flip(index, bit):
    return index + bit * (1 - 2 * lax.rem(lax.div(index, bit), 2))


def place(slot, count):
    return slot // 2 + (slot % 2) * (count // 2)


def greet(bits, hid_count):
    req, hid = lax.axis_index("req"), lax.axis_index("hid")
    barrier = pltpu.get_barrier_semaphore()
    for bit in bits:
        pl.semaphore_signal(barrier, inc=1, device_id=(flip(req, bit), hid), device_id_type=MESH)
    for step in range(1, hid_count):
        other = lax.rem(hid + step, hid_count)
        pl.semaphore_signal(barrier, inc=1, device_id=(req, other), device_id_type=MESH)
    return lambda: pl.semaphore_wait(barrier, len(bits) + hid_count - 1)


def reduce_orders(req_count):
    bits = [1 << i for i in range(req_count.bit_length() - 1)]
    return [bits if c % 2 == 0 else bits[:1] + bits[:0:-1] for c in range(CHUNKS)]


def gather_kernel(
    req_count, hid_count, tok_ref, gain_ref, table_ref, w_hbm, qkv_hbm, qkv_ref, hidden_ref,
    full, w_ref, qkv_w, total, hid_send, hid_recv, req_send, req_recv, w_sem, qkv_sem,
):
    req, hid = lax.axis_index("req"), lax.axis_index("hid")
    orders = [order[::-1] for order in reduce_orders(req_count)]
    width = tok_ref.shape[1] // CHUNKS
    half = req_count // 2
    greeted = greet(orders[0], hid_count)
    qkv_copies = []
    for j in range(3):
        copy = pltpu.make_async_copy(qkv_hbm.at[j], qkv_w.at[j], qkv_sem.at[j])
        copy.start()
        qkv_copies.append(copy)
    w_copy = pltpu.make_async_copy(w_hbm, w_ref, w_sem)
    w_copy.start()
    _, requests, heads, request_rows, _ = qkv_ref.shape
    own = request_rows // hid_count
    pieces = [(j, head) for j in range(3) for head in range(heads)]

    def project_one():
        j, head = pieces.pop(0)
        if head == 0:
            qkv_copies[j].wait()
        group = full[0].reshape(hid_count * full.shape[2], full.shape[3])
        value = jnp.dot(
            group, qkv_w[j, :, head * HEAD_DIM : (head + 1) * HEAD_DIM],
            preferred_element_type=jnp.float32,
        ).astype(jnp.bfloat16).astype(jnp.float32)
        if j < 2:
            value = turn(value, table_ref[...])
        for r in range(requests):
            rows = [value[(h * requests + r) * own : (h * requests + r + 1) * own] for h in range(hid_count)]
            qkv_ref[j, r, head] = jnp.concatenate(rows, axis=0).astype(qkv_ref.dtype)

    values = tok_ref[...].astype(jnp.float32)
    full[0, hid] = layer_norm(values, gain_ref[...]).astype(full.dtype)
    greeted()
    columns = [pl.ds(c * width, width) for c in range(CHUNKS)]
    sent = []
    arriving = [[] for _ in range(CHUNKS)]
    for c in range(CHUNKS):
        for step in range(1, hid_count):
            block = full.at[0, hid, :, columns[c]]
            copy = pltpu.make_async_remote_copy(
                src_ref=block, dst_ref=block,
                send_sem=hid_send.at[c, step - 1], recv_sem=hid_recv.at[c, step - 1],
                device_id=(req, lax.rem(hid + step, hid_count)), device_id_type=MESH,
            )
            copy.start()
            sent.append(copy)
            arriving[c].append(copy)
    held = [[0] for _ in range(CHUNKS)]
    for stage in range(len(orders[0])):
        for c in range(CHUNKS):
            bit = orders[c][stage]
            for copy in arriving[c]:
                copy.wait_recv()
            arriving[c] = []
            for slot in list(held[c]):
                there = slot ^ bit
                copy = pltpu.make_async_remote_copy(
                    src_ref=full.at[place(slot, req_count), :, :, columns[c]],
                    dst_ref=full.at[place(there, req_count), :, :, columns[c]],
                    send_sem=req_send.at[c, there - 1], recv_sem=req_recv.at[c, there - 1],
                    device_id=(flip(req, bit), hid), device_id_type=MESH,
                )
                copy.start()
                sent.append(copy)
                arriving[c].append(copy)
                held[c].append(there)
            if stage > 0 and pieces:
                project_one()
        if stage == 0:
            while len(pieces) > CHUNKS * (len(orders[0]) - 1):
                project_one()
    while pieces:
        project_one()
    w_copy.wait()
    rows = half * full.shape[1] * full.shape[2]
    for side in range(2):
        for c in range(CHUNKS):
            if side == 1:
                for copy in arriving[c]:
                    copy.wait_recv()
            block = full[side * half : (side + 1) * half, :, :, c * width : (c + 1) * width]
            part = jnp.dot(
                block.reshape(rows, width), w_ref[c * width : (c + 1) * width, :],
                preferred_element_type=jnp.float32,
            )
            total[...] = part if c == 0 else total[...] + part
        hidden_ref[side] = jax.nn.gelu(total[...], approximate=True).astype(hidden_ref.dtype)
    for copy in sent:
        copy.wait_send()


def reduce_kernel(
    req_count, hid_count, lengths_ref, bounds_ref, hidden_ref, qkv_ref,
    w_hbm, keys_hbm, values_hbm, tail_keys_hbm, tail_values_hbm, out_hbm, out_ref,
    w_ref, keys, values, tail_keys, tail_values, out_w, attended,
    part, landed, total, leaving, hid_landed,
    w_sem, cache_sem, out_sem, req_send, req_recv, hid_send, hid_recv,
):
    req, hid = lax.axis_index("req"), lax.axis_index("hid")
    orders = reduce_orders(req_count)
    half = req_count // 2
    width = part.shape[-1]
    block_shape = (half,) + part.shape[2:]
    greeted = greet(orders[0], hid_count)
    w_copies = []
    for c in range(CHUNKS):
        copy = pltpu.make_async_copy(
            w_hbm.at[:, pl.ds(c * width, width)], w_ref.at[c], w_sem.at[c]
        )
        copy.start()
        w_copies.append(copy)
    _, requests, heads, request_rows, _ = qkv_ref.shape
    own = request_rows // hid_count
    cache_copies = []
    for r in range(requests):
        pairs = (
            (keys_hbm, keys), (tail_keys_hbm, tail_keys), (values_hbm, values), (tail_values_hbm, tail_values),
        )
        for i, (source, target) in enumerate(pairs):
            copy = pltpu.make_async_copy(source.at[r], target.at[r], cache_sem.at[r, i])
            copy.start()
            cache_copies.append(copy)
    out_copy = pltpu.make_async_copy(out_hbm, out_w, out_sem)
    out_copy.start()
    units = [(r, head) for r in range(requests) for head in range(heads)]

    def scores_of(query, some_keys):
        return lax.dot_general(
            query, some_keys, (((1,), (1,)), ((), ())), preferred_element_type=jnp.float32
        ) * HEAD_DIM ** (-0.5)

    def attend_one():
        r, head = units.pop(0)
        if head == 0:
            for copy in cache_copies[4 * r : 4 * r + 4]:
                copy.wait()
        at = slice(head * HEAD_DIM, (head + 1) * HEAD_DIM)
        query = qkv_ref[0, r, head]
        prompt = scores_of(query, keys[r, :, at])
        tail = scores_of(query, tail_keys[r, :, at])
        fresh = scores_of(query, qkv_ref[1, r, head])
        bounds = bounds_ref[r]
        spot = lax.broadcasted_iota(jnp.int32, prompt.shape, 1)
        prompt = jnp.where(spot < lengths_ref[r], prompt, very_low)
        spot = lax.broadcasted_iota(jnp.int32, tail.shape, 1)
        tail = jnp.where((spot >= bounds[:, 0:1]) & (spot < bounds[:, 1:2]), tail, very_low)
        spot = lax.broadcasted_iota(jnp.int32, fresh.shape, 1)
        fresh = jnp.where((spot >= bounds[:, 2:3]) & (spot <= bounds[:, 3:4]), fresh, very_low)
        highest = functools.reduce(
            jnp.maximum, [jnp.max(some, axis=1, keepdims=True) for some in (prompt, tail, fresh)]
        )
        totals, accrued = 0.0, 0.0
        for some, some_values in (
            (prompt, values[r, :, at]), (tail, tail_values[r, :, at]), (fresh, qkv_ref[2, r, head]),
        ):
            weights = jnp.exp(some - highest)
            totals = totals + jnp.sum(weights, axis=1, keepdims=True)
            accrued = accrued + jnp.dot(
                weights.astype(jnp.bfloat16), some_values, preferred_element_type=jnp.float32
            )
        attended[r * request_rows : (r + 1) * request_rows, at] = (accrued / totals).astype(
            attended.dtype
        )

    sent = []

    def send(c, slot, bit):
        copy = pltpu.make_async_remote_copy(
            src_ref=part.at[c, place(slot, req_count)], dst_ref=landed.at[c, slot - 1],
            send_sem=req_send.at[c, slot - 1], recv_sem=req_recv.at[c, slot - 1],
            device_id=(flip(req, bit), hid), device_id_type=MESH,
        )
        copy.start()
        sent.append(copy)
        return copy

    active = [list(range(req_count)) for _ in range(CHUNKS)]
    arriving = [{} for _ in range(CHUNKS)]
    for c in range(CHUNKS):
        w_copies[c].wait()
        for side in (1, 0):
            value = jnp.dot(hidden_ref[side], w_ref[c], preferred_element_type=jnp.float32)
            part[c, side * half : (side + 1) * half] = value.astype(part.dtype).reshape(block_shape)
            if side == 1:
                if c == 0:
                    greeted()
                for slot in range(1, req_count, 2):
                    arriving[c][slot] = send(c, slot, 1)
        active[c] = list(range(0, req_count, 2))
    for stage in range(1, len(orders[0])):
        for c in range(CHUNKS):
            before, bit = orders[c][stage - 1], orders[c][stage]
            landing, arriving[c] = arriving[c], {}
            for slot in sorted(active[c], key=lambda s: -(s & bit)):
                landing[slot | before].wait_recv()
                at = place(slot, req_count)
                both = part[c, at].astype(jnp.float32) + landed[c, (slot | before) - 1].astype(
                    jnp.float32
                )
                part[c, at] = both.astype(part.dtype)
                if slot & bit:
                    arriving[c][slot] = send(c, slot, bit)
            active[c] = [slot for slot in active[c] if not slot & bit]
            if units:
                attend_one()
    while units:
        attend_one()
    out_copy.wait()
    hid_copies = []
    for c in range(CHUNKS):
        last = orders[c][-1]
        projected = jnp.dot(
            attended[...], out_w[:, c * width : (c + 1) * width], preferred_element_type=jnp.float32
        )
        spans = [
            projected[r * request_rows + h * own : r * request_rows + (h + 1) * own]
            for h in range(hid_count)
            for r in range(requests)
        ]
        arriving[c][last].wait_recv()
        both = part[c, 0].astype(jnp.float32) + landed[c, last - 1].astype(jnp.float32)
        both = both + jnp.concatenate(spans, axis=0).reshape(both.shape)
        total[c] = both
        leaving[c] = both.astype(leaving.dtype)
        for step in range(1, hid_count):
            other = lax.rem(hid + step, hid_count)
            copy = pltpu.make_async_remote_copy(
                src_ref=leaving.at[c, other], dst_ref=hid_landed.at[c, step - 1],
                send_sem=hid_send.at[c, step - 1], recv_sem=hid_recv.at[c, step - 1],
                device_id=(req, other), device_id_type=MESH,
            )
            copy.start()
            sent.append(copy)
            hid_copies.append(copy)
    for c in range(CHUNKS):
        value = total[c, hid]
        for step in range(1, hid_count):
            hid_copies[c * (hid_count - 1) + step - 1].wait_recv()
            value = value + hid_landed[c, step - 1].astype(jnp.float32)
        out_ref[:, c * width : (c + 1) * width] = value
    for copy in sent:
        copy.wait_send()


def in_vmem(count):
    return [pl.BlockSpec(memory_space=pltpu.VMEM)] * count


def params(collective_id):
    return pltpu.CompilerParams(
        collective_id=collective_id, has_side_effects=True, vmem_limit_bytes=58 * 2**20
    )


def gather_up(own_tokens, gain, table, in_weight, qkv_weight, requests):
    req_count, hid_count = lax.axis_size("req"), lax.axis_size("hid")
    rows, width = own_tokens.shape
    units = in_weight.shape[1]
    slab = qkv_weight.shape[2]
    side_rows = req_count // 2 * hid_count * rows
    dma = pltpu.SemaphoreType.DMA
    return pl.pallas_call(
        functools.partial(gather_kernel, req_count, hid_count),
        out_shape=(
            jax.ShapeDtypeStruct(
                (3, requests, slab // HEAD_DIM, hid_count * rows // requests, HEAD_DIM), jnp.bfloat16
            ),
            jax.ShapeDtypeStruct((2, side_rows, units), jnp.bfloat16),
        ),
        in_specs=in_vmem(3) + [pl.BlockSpec(memory_space=pl.ANY)] * 2,
        out_specs=tuple(in_vmem(2)),
        scratch_shapes=[
            pltpu.VMEM((req_count, hid_count, rows, width), jnp.bfloat16),
            pltpu.VMEM((width, units), jnp.bfloat16),
            pltpu.VMEM(qkv_weight.shape, jnp.bfloat16),
            pltpu.VMEM((side_rows, units), jnp.float32),
            dma((CHUNKS, hid_count - 1)),
            dma((CHUNKS, hid_count - 1)),
            dma((CHUNKS, req_count - 1)),
            dma((CHUNKS, req_count - 1)),
            dma(()),
            dma((3,)),
        ],
        compiler_params=params(0),
        name="gather_up",
    )(own_tokens, gain.reshape(1, width), table, in_weight, qkv_weight)


def down_reduce(rows, lengths, bounds, hidden_units, qkv, down_weight, caches, out_weight):
    req_count, hid_count = lax.axis_size("req"), lax.axis_size("hid")
    units, width = down_weight.shape
    part_width = width // CHUNKS
    dma = pltpu.SemaphoreType.DMA
    return pl.pallas_call(
        functools.partial(reduce_kernel, req_count, hid_count),
        out_shape=jax.ShapeDtypeStruct((rows, width), jnp.float32),
        in_specs=[pl.BlockSpec(memory_space=pltpu.SMEM)]
        + in_vmem(3)
        + [pl.BlockSpec(memory_space=pl.ANY)] * 6,
        out_specs=in_vmem(1)[0],
        scratch_shapes=[
            pltpu.VMEM((CHUNKS, units, part_width), jnp.bfloat16),
            *(pltpu.VMEM(cache.shape, jnp.bfloat16) for cache in caches),
            pltpu.VMEM(out_weight.shape, jnp.bfloat16),
            pltpu.VMEM((hid_count * rows, out_weight.shape[0]), jnp.bfloat16),
            pltpu.VMEM((CHUNKS, req_count, hid_count, rows, part_width), jnp.bfloat16),
            pltpu.VMEM((CHUNKS, req_count - 1, hid_count, rows, part_width), jnp.bfloat16),
            pltpu.VMEM((CHUNKS, hid_count, rows, part_width), jnp.float32),
            pltpu.VMEM((CHUNKS, hid_count, rows, part_width), jnp.bfloat16),
            pltpu.VMEM((CHUNKS, hid_count - 1, rows, part_width), jnp.bfloat16),
            dma((CHUNKS,)),
            dma((lengths.shape[0], 4)),
            dma(()),
            dma((CHUNKS, req_count - 1)),
            dma((CHUNKS, req_count - 1)),
            dma((CHUNKS, hid_count - 1)),
            dma((CHUNKS, hid_count - 1)),
        ],
        compiler_params=params(1),
        name="down_reduce",
    )(lengths, bounds, hidden_units, qkv, down_weight, *caches, out_weight)


def shards(
    tokens,
    input_gain,
    qkv_weight,
    out_weight,
    in_weight,
    down_weight,
    final_gain,
    score_weight,
    prompt_keys,
    prompt_values,
    tail_keys,
    tail_values,
    prompt_lengths,
    tail_lengths,
):
    req_dev, samp_dev, fresh, width = tokens.shape
    own_rows = req_dev * samp_dev * fresh
    own_tokens = tokens.reshape(own_rows, width)
    residual = own_tokens.astype(jnp.float32)
    hid_count = lax.axis_size("hid")
    samples = hid_count * samp_dev
    positions = (
        prompt_lengths[:, None, None]
        + tail_lengths[:, :, None]
        + jnp.arange(fresh, dtype=jnp.int32)[None, None, :]
    )
    row_positions = jnp.transpose(
        positions.reshape(req_dev, hid_count, samp_dev, fresh), (1, 0, 2, 3)
    ).reshape(hid_count * own_rows)
    qkv, hidden_units = gather_up(
        own_tokens, input_gain, rotation_table(row_positions), in_weight,
        jnp.transpose(qkv_weight, (1, 0, 2)), req_dev,
    )
    tail_len, slab = tail_keys.shape[2:]
    row = jnp.arange(samples * fresh, dtype=jnp.int32)
    sample = row // fresh
    first_tail = jnp.broadcast_to(sample * tail_len, (req_dev, samples * fresh))
    bounds = jnp.stack(
        [
            first_tail,
            first_tail + jnp.repeat(tail_lengths, fresh, axis=1),
            jnp.broadcast_to(sample * fresh, first_tail.shape),
            jnp.broadcast_to(row, first_tail.shape),
        ],
        axis=-1,
    )
    caches = (
        prompt_keys,
        prompt_values,
        tail_keys.reshape(req_dev, samples * tail_len, slab),
        tail_values.reshape(req_dev, samples * tail_len, slab),
    )
    branch_sum = down_reduce(
        own_rows, prompt_lengths, bounds, hidden_units, qkv, down_weight, caches, out_weight
    )
    final_state = residual + branch_sum
    next_hidden = final_state.astype(jnp.bfloat16).reshape(req_dev, samp_dev, fresh, width)
    sample_scores = jnp.sum(
        layer_norm(final_state, final_gain) * score_weight.astype(jnp.float32), axis=-1
    )
    return (next_hidden, sample_scores.reshape(req_dev, samp_dev, fresh))


def solution(mesh):
    placed = (
        P("req", "hid", None, None),
        P(),
        P(None, None, "hid"),
        P("hid", None),
        P(None, ("req", "hid")),
        P(("req", "hid"), None),
        P(),
        P(),
        P("req", None, "hid"),
        P("req", None, "hid"),
        P("req", None, None, "hid"),
        P("req", None, None, "hid"),
        P("req"),
        P("req", None),
    )
    return jax.shard_map(
        shards,
        mesh=mesh,
        in_specs=placed,
        out_specs=(P("req", "hid", None, None), P("req", "hid", None)),
        check_vma=False,
    )
```

```python
import functools

import jax
import jax.numpy as jnp
from jax import lax
from jax.experimental import pallas as pl
from jax.experimental.pallas import tpu as pltpu
from jax.sharding import PartitionSpec as P

HEAD_DIM = 256
ROT = 64


very_low = -1e30


def layer_norm(values, gain):
    centre = jnp.mean(values, axis=-1, keepdims=True)
    centred = values - centre
    spread = jnp.mean(centred * centred, axis=-1, keepdims=True)
    return centred * lax.rsqrt(spread + 1e-05) * gain


def turn(vectors, table):
    lanes = table.shape[-1]
    first = vectors[:, :lanes]
    even = lax.rem(lax.broadcasted_iota(jnp.int32, first.shape, 1), 2) == 0
    other = jnp.where(even, pltpu.roll(first, lanes - 1, 1), pltpu.roll(first, 1, 1))
    return jnp.concatenate([first * table[0] + other * table[1], vectors[:, lanes:]], axis=1)


def rotation_table(positions):
    lane = jnp.arange(2 * ROT, dtype=jnp.int32)
    frequency = 10000.0 ** (-((lane // 2).astype(jnp.float32) * (2.0 / ROT)))
    angles = positions.astype(jnp.float32)[:, None] * jnp.where(lane < ROT, frequency, 0.0)
    sign = jnp.where(lane % 2 == 0, -1.0, 1.0)
    return jnp.stack([jnp.cos(angles), jnp.sin(angles) * sign])


CHUNKS = 4
MESH = pl.DeviceIdType.MESH


def flip(index, bit):
    return index + bit * (1 - 2 * lax.rem(lax.div(index, bit), 2))


def place(slot, count):
    return slot // 2 + (slot % 2) * (count // 2)


def greet(bits, hid_count):
    req, hid = lax.axis_index("req"), lax.axis_index("hid")
    barrier = pltpu.get_barrier_semaphore()
    for bit in bits:
        pl.semaphore_signal(barrier, inc=1, device_id=(flip(req, bit), hid), device_id_type=MESH)
    for step in range(1, hid_count):
        other = lax.rem(hid + step, hid_count)
        pl.semaphore_signal(barrier, inc=1, device_id=(req, other), device_id_type=MESH)
    return lambda: pl.semaphore_wait(barrier, len(bits) + hid_count - 1)


def reduce_orders(req_count):
    bits = [1 << i for i in range(req_count.bit_length() - 1)]
    return [bits if c % 2 == 0 else bits[:1] + bits[:0:-1] for c in range(CHUNKS)]


def gather_kernel(
    req_count, hid_count, tok_ref, gain_ref, table_ref, w_hbm, qkv_hbm, qkv_ref, hidden_ref,
    full, w_ref, qkv_w, qkv_total, total, hid_send, hid_recv, req_send, req_recv, w_sem, qkv_sem,
):
    req, hid = lax.axis_index("req"), lax.axis_index("hid")
    orders = [order[::-1] for order in reduce_orders(req_count)]
    width = tok_ref.shape[1] // CHUNKS
    half = req_count // 2
    greeted = greet(orders[0], hid_count)
    qkv_copies = []
    for j in range(3):
        copy = pltpu.make_async_copy(qkv_hbm.at[j], qkv_w.at[j], qkv_sem.at[j])
        copy.start()
        qkv_copies.append(copy)
    w_copy = pltpu.make_async_copy(w_hbm, w_ref, w_sem)
    w_copy.start()
    _, requests, heads, request_rows, _ = qkv_ref.shape
    own = request_rows // hid_count
    pieces = [(c, j) for c in range(CHUNKS) for j in range(3)]
    piece_count = len(pieces)

    def project_one():
        c, j = pieces.pop(0)
        if c == 0:
            qkv_copies[j].wait()
        group = full[0, :, :, c * width : (c + 1) * width].reshape(hid_count * full.shape[2], width)
        value = jnp.dot(
            group, qkv_w[j, c * width : (c + 1) * width, :], preferred_element_type=jnp.float32
        )
        if c > 0:
            value = value + qkv_total[j]
        if c < CHUNKS - 1:
            qkv_total[j] = value
            return
        value = value.astype(jnp.bfloat16).astype(jnp.float32)
        for head in range(heads):
            part = value[:, head * HEAD_DIM : (head + 1) * HEAD_DIM]
            if j < 2:
                part = turn(part, table_ref[...])
            for r in range(requests):
                rows = [
                    part[(h * requests + r) * own : (h * requests + r + 1) * own]
                    for h in range(hid_count)
                ]
                qkv_ref[j, r, head] = jnp.concatenate(rows, axis=0).astype(qkv_ref.dtype)

    values = tok_ref[...].astype(jnp.float32)
    full[0, hid] = layer_norm(values, gain_ref[...]).astype(full.dtype)
    greeted()
    columns = [pl.ds(c * width, width) for c in range(CHUNKS)]
    sent = []
    arriving = [[] for _ in range(CHUNKS)]
    for c in range(CHUNKS):
        for step in range(1, hid_count):
            block = full.at[0, hid, :, columns[c]]
            copy = pltpu.make_async_remote_copy(
                src_ref=block, dst_ref=block,
                send_sem=hid_send.at[c, step - 1], recv_sem=hid_recv.at[c, step - 1],
                device_id=(req, lax.rem(hid + step, hid_count)), device_id_type=MESH,
            )
            copy.start()
            sent.append(copy)
            arriving[c].append(copy)
    held = [[0] for _ in range(CHUNKS)]
    for stage in range(len(orders[0])):
        for c in range(CHUNKS):
            bit = orders[c][stage]
            for copy in arriving[c]:
                copy.wait_recv()
            arriving[c] = []
            for slot in list(held[c]):
                there = slot ^ bit
                copy = pltpu.make_async_remote_copy(
                    src_ref=full.at[place(slot, req_count), :, :, columns[c]],
                    dst_ref=full.at[place(there, req_count), :, :, columns[c]],
                    send_sem=req_send.at[c, there - 1], recv_sem=req_recv.at[c, there - 1],
                    device_id=(flip(req, bit), hid), device_id_type=MESH,
                )
                copy.start()
                sent.append(copy)
                arriving[c].append(copy)
                held[c].append(there)
            if stage == 0:
                while len(pieces) > piece_count - 2 * (c + 1):
                    project_one()
            elif pieces:
                project_one()
    while pieces:
        project_one()
    w_copy.wait()
    rows = half * full.shape[1] * full.shape[2]
    for side in range(2):
        for c in range(CHUNKS):
            if side == 1:
                for copy in arriving[c]:
                    copy.wait_recv()
            block = full[side * half : (side + 1) * half, :, :, c * width : (c + 1) * width]
            part = jnp.dot(
                block.reshape(rows, width), w_ref[c * width : (c + 1) * width, :],
                preferred_element_type=jnp.float32,
            )
            total[...] = part if c == 0 else total[...] + part
        hidden_ref[side] = jax.nn.gelu(total[...], approximate=True).astype(hidden_ref.dtype)
    for copy in sent:
        copy.wait_send()


def reduce_kernel(
    req_count, hid_count, lengths_ref, bounds_ref, tok_ref, gain_ref, score_w_ref, hidden_ref, qkv_ref,
    w_hbm, keys_hbm, values_hbm, tail_keys_hbm, tail_values_hbm, out_hbm, next_ref, score_ref,
    state,
    w_ref, keys, values, tail_keys, tail_values, out_w, attended,
    part, landed, total, leaving, hid_landed,
    w_sem, cache_sem, out_sem, req_send, req_recv, hid_send, hid_recv,
):
    req, hid = lax.axis_index("req"), lax.axis_index("hid")
    orders = reduce_orders(req_count)
    half = req_count // 2
    width = part.shape[-1]
    block_shape = (half,) + part.shape[2:]
    greeted = greet(orders[0], hid_count)
    w_copies = []
    for c in range(CHUNKS):
        copy = pltpu.make_async_copy(
            w_hbm.at[:, pl.ds(c * width, width)], w_ref.at[c], w_sem.at[c]
        )
        copy.start()
        w_copies.append(copy)
    _, requests, heads, request_rows, _ = qkv_ref.shape
    own = request_rows // hid_count
    cache_copies = []
    for r in range(requests):
        pairs = (
            (keys_hbm, keys), (tail_keys_hbm, tail_keys), (values_hbm, values), (tail_values_hbm, tail_values),
        )
        for i, (source, target) in enumerate(pairs):
            copy = pltpu.make_async_copy(source.at[r], target.at[r], cache_sem.at[r, i])
            copy.start()
            cache_copies.append(copy)
    out_copy = pltpu.make_async_copy(out_hbm, out_w, out_sem)
    out_copy.start()
    units = [(r, head) for r in range(requests) for head in range(heads)]

    def scores_of(query, some_keys):
        return lax.dot_general(
            query, some_keys, (((1,), (1,)), ((), ())), preferred_element_type=jnp.float32
        ) * HEAD_DIM ** (-0.5)

    def attend_one():
        r, head = units.pop(0)
        if head == 0:
            for copy in cache_copies[4 * r : 4 * r + 4]:
                copy.wait()
        at = slice(head * HEAD_DIM, (head + 1) * HEAD_DIM)
        query = qkv_ref[0, r, head]
        prompt = scores_of(query, keys[r, :, at])
        tail = scores_of(query, tail_keys[r, :, at])
        fresh = scores_of(query, qkv_ref[1, r, head])
        bounds = bounds_ref[r]
        spot = lax.broadcasted_iota(jnp.int32, prompt.shape, 1)
        prompt = jnp.where(spot < lengths_ref[r], prompt, very_low)
        spot = lax.broadcasted_iota(jnp.int32, tail.shape, 1)
        tail = jnp.where((spot >= bounds[:, 0:1]) & (spot < bounds[:, 1:2]), tail, very_low)
        spot = lax.broadcasted_iota(jnp.int32, fresh.shape, 1)
        fresh = jnp.where((spot >= bounds[:, 2:3]) & (spot <= bounds[:, 3:4]), fresh, very_low)
        highest = functools.reduce(
            jnp.maximum, [jnp.max(some, axis=1, keepdims=True) for some in (prompt, tail, fresh)]
        )
        totals, accrued = 0.0, 0.0
        for some, some_values in (
            (prompt, values[r, :, at]), (tail, tail_values[r, :, at]), (fresh, qkv_ref[2, r, head]),
        ):
            weights = jnp.exp(some - highest)
            totals = totals + jnp.sum(weights, axis=1, keepdims=True)
            accrued = accrued + jnp.dot(
                weights.astype(jnp.bfloat16), some_values, preferred_element_type=jnp.float32
            )
        attended[r * request_rows : (r + 1) * request_rows, at] = (accrued / totals).astype(
            attended.dtype
        )

    sent = []

    def send(c, slot, bit):
        copy = pltpu.make_async_remote_copy(
            src_ref=part.at[c, place(slot, req_count)], dst_ref=landed.at[c, slot - 1],
            send_sem=req_send.at[c, slot - 1], recv_sem=req_recv.at[c, slot - 1],
            device_id=(flip(req, bit), hid), device_id_type=MESH,
        )
        copy.start()
        sent.append(copy)
        return copy

    active = [list(range(req_count)) for _ in range(CHUNKS)]
    arriving = [{} for _ in range(CHUNKS)]
    for c in range(CHUNKS):
        w_copies[c].wait()
        for side in (1, 0):
            value = jnp.dot(hidden_ref[side], w_ref[c], preferred_element_type=jnp.float32)
            part[c, side * half : (side + 1) * half] = value.astype(part.dtype).reshape(block_shape)
            if side == 1:
                if c == 0:
                    greeted()
                for slot in range(1, req_count, 2):
                    arriving[c][slot] = send(c, slot, 1)
        active[c] = list(range(0, req_count, 2))
    for stage in range(1, len(orders[0])):
        for c in range(CHUNKS):
            before, bit = orders[c][stage - 1], orders[c][stage]
            landing, arriving[c] = arriving[c], {}
            for slot in sorted(active[c], key=lambda s: -(s & bit)):
                landing[slot | before].wait_recv()
                at = place(slot, req_count)
                both = part[c, at].astype(jnp.float32) + landed[c, (slot | before) - 1].astype(
                    jnp.float32
                )
                part[c, at] = both.astype(part.dtype)
                if slot & bit:
                    arriving[c][slot] = send(c, slot, bit)
            active[c] = [slot for slot in active[c] if not slot & bit]
            if units:
                attend_one()
    while units:
        attend_one()
    out_copy.wait()
    hid_copies = []
    for c in range(CHUNKS):
        last = orders[c][-1]
        projected = jnp.dot(
            attended[...], out_w[:, c * width : (c + 1) * width], preferred_element_type=jnp.float32
        )
        spans = [
            projected[r * request_rows + h * own : r * request_rows + (h + 1) * own]
            for h in range(hid_count)
            for r in range(requests)
        ]
        arriving[c][last].wait_recv()
        both = part[c, 0].astype(jnp.float32) + landed[c, last - 1].astype(jnp.float32)
        both = both + jnp.concatenate(spans, axis=0).reshape(both.shape)
        total[c] = both
        leaving[c] = both.astype(leaving.dtype)
        for step in range(1, hid_count):
            other = lax.rem(hid + step, hid_count)
            copy = pltpu.make_async_remote_copy(
                src_ref=leaving.at[c, other], dst_ref=hid_landed.at[c, step - 1],
                send_sem=hid_send.at[c, step - 1], recv_sem=hid_recv.at[c, step - 1],
                device_id=(req, other), device_id_type=MESH,
            )
            copy.start()
            sent.append(copy)
            hid_copies.append(copy)
    for c in range(CHUNKS):
        value = total[c, hid]
        for step in range(1, hid_count):
            hid_copies[c * (hid_count - 1) + step - 1].wait_recv()
            value = value + hid_landed[c, step - 1].astype(jnp.float32)
        at = slice(c * width, (c + 1) * width)
        value = value + tok_ref[:, at].astype(jnp.float32)
        state[:, at] = value
        next_ref[:, at] = value.astype(next_ref.dtype)
    scored = layer_norm(state[...], gain_ref[...]) * score_w_ref[...].astype(jnp.float32)
    score_ref[...] = jnp.broadcast_to(jnp.sum(scored, axis=-1, keepdims=True), score_ref.shape)
    for copy in sent:
        copy.wait_send()


def in_vmem(count):
    return [pl.BlockSpec(memory_space=pltpu.VMEM)] * count


def params(collective_id):
    return pltpu.CompilerParams(
        collective_id=collective_id, has_side_effects=True, vmem_limit_bytes=58 * 2**20
    )


def gather_up(own_tokens, gain, table, in_weight, qkv_weight, requests):
    req_count, hid_count = lax.axis_size("req"), lax.axis_size("hid")
    rows, width = own_tokens.shape
    units = in_weight.shape[1]
    slab = qkv_weight.shape[2]
    side_rows = req_count // 2 * hid_count * rows
    dma = pltpu.SemaphoreType.DMA
    return pl.pallas_call(
        functools.partial(gather_kernel, req_count, hid_count),
        out_shape=(
            jax.ShapeDtypeStruct(
                (3, requests, slab // HEAD_DIM, hid_count * rows // requests, HEAD_DIM), jnp.bfloat16
            ),
            jax.ShapeDtypeStruct((2, side_rows, units), jnp.bfloat16),
        ),
        in_specs=in_vmem(3) + [pl.BlockSpec(memory_space=pl.ANY)] * 2,
        out_specs=tuple(in_vmem(2)),
        scratch_shapes=[
            pltpu.VMEM((req_count, hid_count, rows, width), jnp.bfloat16),
            pltpu.VMEM((width, units), jnp.bfloat16),
            pltpu.VMEM(qkv_weight.shape, jnp.bfloat16),
            pltpu.VMEM((3, hid_count * rows, slab), jnp.float32),
            pltpu.VMEM((side_rows, units), jnp.float32),
            dma((CHUNKS, hid_count - 1)),
            dma((CHUNKS, hid_count - 1)),
            dma((CHUNKS, req_count - 1)),
            dma((CHUNKS, req_count - 1)),
            dma(()),
            dma((3,)),
        ],
        compiler_params=params(0),
        name="gather_up",
    )(own_tokens, gain.reshape(1, width), table, in_weight, qkv_weight)


def down_reduce(own_tokens, gain, score_weight, lengths, bounds, hidden_units, qkv, down_weight, caches, out_weight):
    req_count, hid_count = lax.axis_size("req"), lax.axis_size("hid")
    units, width = down_weight.shape
    rows = own_tokens.shape[0]
    part_width = width // CHUNKS
    dma = pltpu.SemaphoreType.DMA
    return pl.pallas_call(
        functools.partial(reduce_kernel, req_count, hid_count),
        out_shape=(
            jax.ShapeDtypeStruct((rows, width), jnp.bfloat16),
            jax.ShapeDtypeStruct((rows, 128), jnp.float32),
        ),
        in_specs=[pl.BlockSpec(memory_space=pltpu.SMEM)]
        + in_vmem(6)
        + [pl.BlockSpec(memory_space=pl.ANY)] * 6,
        out_specs=tuple(in_vmem(2)),
        scratch_shapes=[
            pltpu.VMEM((rows, width), jnp.float32),
            pltpu.VMEM((CHUNKS, units, part_width), jnp.bfloat16),
            *(pltpu.VMEM(cache.shape, jnp.bfloat16) for cache in caches),
            pltpu.VMEM(out_weight.shape, jnp.bfloat16),
            pltpu.VMEM((hid_count * rows, out_weight.shape[0]), jnp.bfloat16),
            pltpu.VMEM((CHUNKS, req_count, hid_count, rows, part_width), jnp.bfloat16),
            pltpu.VMEM((CHUNKS, req_count - 1, hid_count, rows, part_width), jnp.bfloat16),
            pltpu.VMEM((CHUNKS, hid_count, rows, part_width), jnp.float32),
            pltpu.VMEM((CHUNKS, hid_count, rows, part_width), jnp.bfloat16),
            pltpu.VMEM((CHUNKS, hid_count - 1, rows, part_width), jnp.bfloat16),
            dma((CHUNKS,)),
            dma((lengths.shape[0], 4)),
            dma(()),
            dma((CHUNKS, req_count - 1)),
            dma((CHUNKS, req_count - 1)),
            dma((CHUNKS, hid_count - 1)),
            dma((CHUNKS, hid_count - 1)),
        ],
        compiler_params=params(1),
        name="down_reduce",
    )(
        lengths, bounds, own_tokens, gain.reshape(1, width), score_weight.reshape(1, width),
        hidden_units, qkv, down_weight, *caches, out_weight,
    )


def shards(
    tokens,
    input_gain,
    qkv_weight,
    out_weight,
    in_weight,
    down_weight,
    final_gain,
    score_weight,
    prompt_keys,
    prompt_values,
    tail_keys,
    tail_values,
    prompt_lengths,
    tail_lengths,
):
    req_dev, samp_dev, fresh, width = tokens.shape
    own_rows = req_dev * samp_dev * fresh
    own_tokens = tokens.reshape(own_rows, width)
    hid_count = lax.axis_size("hid")
    samples = hid_count * samp_dev
    positions = (
        prompt_lengths[:, None, None]
        + tail_lengths[:, :, None]
        + jnp.arange(fresh, dtype=jnp.int32)[None, None, :]
    )
    row_positions = jnp.transpose(
        positions.reshape(req_dev, hid_count, samp_dev, fresh), (1, 0, 2, 3)
    ).reshape(hid_count * own_rows)
    qkv, hidden_units = gather_up(
        own_tokens, input_gain, rotation_table(row_positions), in_weight,
        jnp.transpose(qkv_weight, (1, 0, 2)), req_dev,
    )
    tail_len, slab = tail_keys.shape[2:]
    row = jnp.arange(samples * fresh, dtype=jnp.int32)
    sample = row // fresh
    first_tail = jnp.broadcast_to(sample * tail_len, (req_dev, samples * fresh))
    bounds = jnp.stack(
        [
            first_tail,
            first_tail + jnp.repeat(tail_lengths, fresh, axis=1),
            jnp.broadcast_to(sample * fresh, first_tail.shape),
            jnp.broadcast_to(row, first_tail.shape),
        ],
        axis=-1,
    )
    caches = (
        prompt_keys,
        prompt_values,
        tail_keys.reshape(req_dev, samples * tail_len, slab),
        tail_values.reshape(req_dev, samples * tail_len, slab),
    )
    next_hidden, sample_scores = down_reduce(
        own_tokens, final_gain, score_weight, prompt_lengths, bounds, hidden_units, qkv,
        down_weight, caches, out_weight,
    )
    next_hidden = next_hidden.reshape(req_dev, samp_dev, fresh, width)
    sample_scores = sample_scores[:, 0]
    return (next_hidden, sample_scores.reshape(req_dev, samp_dev, fresh))


def solution(mesh):
    placed = (
        P("req", "hid", None, None),
        P(),
        P(None, None, "hid"),
        P("hid", None),
        P(None, ("req", "hid")),
        P(("req", "hid"), None),
        P(),
        P(),
        P("req", None, "hid"),
        P("req", None, "hid"),
        P("req", None, None, "hid"),
        P("req", None, None, "hid"),
        P("req"),
        P("req", None),
    )
    return jax.shard_map(
        shards,
        mesh=mesh,
        in_specs=placed,
        out_specs=(P("req", "hid", None, None), P("req", "hid", None)),
        check_vma=False,
    )
```
